32 devices in a mesh: sweep: 2 (over x), cell: 16 (over z, y, core).
Axes of the slice: x: 2, y: 2, z: 4, core: 2. Of those that a mesh axis runs over, the one named last changes fastest.
Arguments:
- populations: float32 [1024, 2, 2048], P(('sweep', 'cell')), parts along dimension 0, may hold values from 0.05 to 0.95
- coherences: float32 [1024, 2, 2048], P(('sweep', 'cell')), parts along dimension 0, may hold values from -0.4 to 0.4
- kernel: bfloat16 [2048, 2048], P('cell'), may hold values from 0 to 0.053710938
- velocity: float32 [2048], replicated, may hold values from 0.2 to 1
- heading: int32 [2048], replicated, may hold values from 0 to 1
- wall_flags: int32 [512], P('cell'), may hold values 0 or 1
- detune: float32 [4096], P('sweep'), parts along dimension 0, may hold values from -2 to 2
Outputs:
- populations_out: float32 [1024, 2, 2048], P(('sweep', 'cell')), parts along dimension 0
- coherences_out: float32 [1024, 2, 2048], P(('sweep', 'cell')), parts along dimension 0
The draws below stay inside these ranges and needn't reach their ends.
There are 2 independent parts, one for each index of `sweep`. The reference program is written for one: setup_inputs(seed, part) draws one part's arguments, and reference() takes and returns one part's arrays. A program takes and returns all parts, laid end to end along the dimension named above; an argument that names none is the same for every part. Nothing has to cross between parts.
Inputs may be any that keep to these rules, and one draw needn't show every extreme that they name: `heading`: 1: the momentum moves toward higher cell indices; 0: toward lower ones. `wall_flags`: 1 marks an absorbing cell.
All inputs are finite; a program needn't handle non-finite values. No bound on the sum of `wall_flags` on one device may be relied on, other than what follows from the above.
Results may differ from the reference program's by a relative error of at most 0.0003.
Values may be sent and summed in bfloat16 or wider, within the bound.
A program may use at most 64 MiB of HBM per device.

```python
import math
import jax
import jax.numpy as jnp
from jax import lax

MOMENTUM_POINTS = 2048
STEPS = 4
SPACE_CELLS = 512


def band_energy():
    position = (jnp.arange(MOMENTUM_POINTS, dtype=jnp.float32) + 0.5) / MOMENTUM_POINTS
    return -jnp.cos(math.pi * position)


def draw_populations(key, part):
    key = jax.random.fold_in(key, 11)
    random_subkey_list = jax.random.split(key, 3)
    energy = band_energy()
    chemical = jax.random.uniform(random_subkey_list[0], (SPACE_CELLS, 1, 1), jnp.float32, -0.5, 0.5)
    lattice_heat_level = jnp.exp(jax.random.uniform(random_subkey_list[1], (SPACE_CELLS, 1, 1), jnp.float32, math.log(0.05), math.log(0.3)))
    surface_disorder = jax.random.uniform(random_subkey_list[2], (SPACE_CELLS, 2, MOMENTUM_POINTS), jnp.float32, 0.5, 1.0)
    band_shift = 0.4 * jnp.arange(2, dtype=jnp.float32)[None, :, None]
    surplus_occupation = energy[None, None, :] + band_shift - chemical
    fermi_dirac_level = jax.nn.sigmoid(-surplus_occupation / lattice_heat_level)
    return 0.05 + 0.9 * fermi_dirac_level * surface_disorder


def draw_coherences(key, part):
    key = jax.random.fold_in(key, 12)
    random_subkey_list = jax.random.split(key, 5)
    energy = band_energy()
    amplitude = jax.random.uniform(random_subkey_list[0], (SPACE_CELLS, 1), jnp.float32, 0.15, 0.35)
    frequency = jax.random.uniform(random_subkey_list[1], (SPACE_CELLS, 1), jnp.float32, 2.0, 5.0)
    low_end = 0.5
    phase_shift = jax.random.uniform(random_subkey_list[2], (SPACE_CELLS, 1), jnp.float32, -math.pi, math.pi)
    real_rough = jax.random.uniform(random_subkey_list[3], (SPACE_CELLS, MOMENTUM_POINTS), jnp.float32, low_end, 1.0)
    imag_rough = jax.random.uniform(random_subkey_list[4], (SPACE_CELLS, MOMENTUM_POINTS), jnp.float32, low_end, 1.0)
    angle_here = frequency * energy[None, :] + phase_shift
    real_part = amplitude * jnp.cos(angle_here) * real_rough
    imag_part = amplitude * jnp.sin(angle_here) * imag_rough
    return jnp.stack([real_part, imag_part], axis=1)


def draw_kernel(key, part):
    key = jax.random.fold_in(key, 13)
    energy = band_energy()
    energy_gap = jnp.abs(energy[:, None] - energy[None, :])
    shell_weight = jnp.exp(-jnp.square((energy_gap - 0.3) / 0.04))
    spread = jnp.exp(jax.random.uniform(key, (MOMENTUM_POINTS, MOMENTUM_POINTS), jnp.float32, math.log(0.03), math.log(30.0)))
    return (3.0 / MOMENTUM_POINTS * spread * (0.02 + shell_weight)).astype(jnp.bfloat16)


def plant(drawn, key, low, largest):
    spot = [jax.random.randint(jax.random.fold_in(key, axis), (), 0, length) for axis, length in enumerate(drawn.shape)]
    widest = drawn.shape.index(max(drawn.shape))
    next_to = spot[:widest] + [(spot[widest] + 1) % drawn.shape[widest]] + spot[widest + 1:]
    return drawn.at[tuple(spot)].set(low).at[tuple(next_to)].set(largest)


def setup_inputs(seed: int = 0, part: int = 0) -> dict:
    seeds = jax.random.split(jax.random.key(seed), 8)
    part_keys = jax.random.split(jax.random.fold_in(seeds[7], part), 8)
    return {
        "populations": draw_populations(jax.random.fold_in(jax.random.fold_in(seeds[7], part), 71), part),
        "coherences": draw_coherences(jax.random.fold_in(jax.random.fold_in(seeds[7], part), 71), part),
        "kernel": draw_kernel(jax.random.fold_in(seeds[7], 71), part),
        "velocity": jnp.clip(jax.random.uniform(seeds[3], (MOMENTUM_POINTS,), jnp.float32, 0.2, 1.0), 0.2, 1.0),
        "heading": plant(jax.random.randint(seeds[4], (MOMENTUM_POINTS,), 0, 2), jax.random.fold_in(seeds[4], 1), 0, 1).astype(jnp.int32),
        "wall_flags": plant((jax.random.randint(seeds[5], (SPACE_CELLS,), 0, 8) < 1).astype(jnp.int32), jax.random.fold_in(seeds[5], 1), 0, 1),
        "detune": jnp.clip(jax.random.uniform(part_keys[6], (MOMENTUM_POINTS,), jnp.float32, -2.0, 2.0), -2.0, 2.0),
    }


TIME_STEP = 0.5
ABSORPTION = 1.0


def upwind(padded, forward):
    cells_here = padded.shape[0] - 6

    def displaced_state(offset):
        return lax.slice_in_dim(padded, 3 + offset, 3 + offset + cells_here, axis=0)

    forward_diff = (-2.0 * displaced_state(-3) + 15.0 * displaced_state(-2) - 60.0 * displaced_state(-1) + 20.0 * displaced_state(0) + 30.0 * displaced_state(1) - 3.0 * displaced_state(2)) / 60.0
    backward_diff = (3.0 * displaced_state(-2) - 30.0 * displaced_state(-1) - 20.0 * displaced_state(0) + 60.0 * displaced_state(1) - 15.0 * displaced_state(2) + 2.0 * displaced_state(3)) / 60.0
    return jnp.where(forward, forward_diff, backward_diff)


def rates(padded, wall_mask, kernel, velocity, forward, detune):
    density = padded[3:-3]
    cells_here = density.shape[0]
    momenta = density.shape[2]
    occupied = density[:, :2]
    coherent = density[:, 2:]
    rounded_state = density.astype(jnp.bfloat16).reshape(cells_here * 4, momenta)
    gain_terms = jnp.dot(rounded_state, kernel.T, preferred_element_type=jnp.float32).reshape(cells_here, 4, momenta)
    empty_states = (1.0 - occupied).astype(jnp.bfloat16).reshape(cells_here * 2, momenta)
    loss_rates = jnp.dot(empty_states, kernel, preferred_element_type=jnp.float32).reshape(cells_here, 2, momenta)
    band_terms = (1.0 - occupied) * gain_terms[:, :2] - occupied * loss_rates
    mean_hole = 1.0 - 0.5 * (occupied[:, 0] + occupied[:, 1])
    damping = 0.5 * (loss_rates[:, 0] + loss_rates[:, 1])
    real_part = coherent[:, 0]
    imag_part = coherent[:, 1]
    new_real = mean_hole * gain_terms[:, 2] - damping * real_part - detune * imag_part
    new_imag = mean_hole * gain_terms[:, 3] - damping * imag_part + detune * real_part
    scattering = jnp.concatenate([band_terms, new_real[:, None], new_imag[:, None]], axis=1)
    advection = -velocity * upwind(padded, forward)
    return advection + scattering - ABSORPTION * wall_mask[:, None, None] * density


def reference(populations, coherences, kernel, velocity, heading, wall_flags, detune):
    density = jnp.concatenate([populations, coherences], axis=1)
    forward = heading > 0
    wall_mask = wall_flags.astype(jnp.float32)
    margin = ((3, 3), (0, 0), (0, 0))
    for outer_step in range(STEPS):
        predictor = density + TIME_STEP * rates(jnp.pad(density, margin), wall_mask, kernel, velocity, forward, detune)
        corrector_rate = rates(jnp.pad(predictor, margin), wall_mask, kernel, velocity, forward, detune)
        density = 0.5 * (density + predictor + TIME_STEP * corrector_rate)
    return density[:, :2], density[:, 2:]
```

```python
import functools

import jax
import jax.numpy as jnp
from jax import lax
from jax.experimental import pallas as pl
from jax.experimental.pallas import tpu as pltpu
from jax.sharding import PartitionSpec as P

STEPS = 4
TIME_STEP = 0.5
ABSORPTION = 1.0
LANES = 128
EDGE = 4
FORWARD = (-2.0, 15.0, -60.0, 20.0, 30.0, -3.0, 0.0)
BACKWARD = (0.0, 3.0, -30.0, -20.0, 60.0, -15.0, 2.0)
CHUNKS = 4
BLOCKS = 4


def fused(n, pop_ref, coh_ref, shard_ref, coef_ref, wall_ref, out_ref,
          kern, kern_t, dens, pred, s_dens, s_pred, e_dens, e_pred, gain, loss,
          halo_out, halo_in, ring_send, ring_recv, sib_send, sib_recv,
          halo_send, halo_recv, local_sem):
    cells = pop_ref.shape[0]
    momenta = shard_ref.shape[1]
    rows = shard_ref.shape[0]
    tiles = momenta // LANES
    width = momenta // CHUNKS
    chips = n // 2
    half = chips // 2
    first = 8
    last = first + cells

    me = lax.axis_index("cell")
    core = me % 2
    chip = me // 2
    sibling = chip * 2 + 1 - core
    odd = chip % 2
    spot = (1 - odd) * (chip // 2) + odd * (chips - 1 - chip // 2)

    def device_at(position):
        late = position // half
        at = (1 - late) * (2 * position) + late * (2 * (chips - 1 - position) + 1)
        return at * 2 + core

    right = device_at((spot + 1) % chips)
    left = device_at((spot + chips - 1) % chips)

    barrier = pltpu.get_barrier_semaphore()
    for other in (right, left, sibling, (me + 1) % n, (me + n - 1) % n):
        pl.semaphore_signal(barrier, inc=1, device_id={"cell": other})
    pl.semaphore_wait(barrier, 5)

    def place(device, chunk):
        return kern.at[pl.ds(pl.multiple_of(device * rows, rows), rows),
                       pl.ds(chunk * width, width)]

    def ring_copy(step, chunk, source):
        rightward = chunk < CHUNKS // 2
        position = (spot + chips - step) % chips if rightward else (spot + step) % chips
        here = place(device_at(position), chunk)
        src = shard_ref.at[:, pl.ds(chunk * width, width)] if source else here
        return pltpu.make_async_remote_copy(
            src_ref=src, dst_ref=here,
            send_sem=ring_send.at[chunk, step], recv_sem=ring_recv.at[chunk, step],
            device_id={"cell": right if rightward else left})

    def ring_arrival(step, chunk):
        rightward = chunk < CHUNKS // 2
        position = (spot + 2 * chips - 1 - step) % chips if rightward else (spot + 1 + step) % chips
        here = place(device_at(position), chunk)
        return here, device_at(position)

    def sib_copy(step, chunk, device, source):
        here = place(device, chunk)
        src = shard_ref.at[:, pl.ds(chunk * width, width)] if source else here
        return pltpu.make_async_remote_copy(
            src_ref=src, dst_ref=here,
            send_sem=sib_send.at[chunk, step], recv_sem=sib_recv.at[chunk, step],
            device_id={"cell": sibling})

    def other_core(device):
        return device + 1 - 2 * core

    for chunk in (0, 2, 1, 3):
        ring_copy(0, chunk, True).start()
    for chunk in range(CHUNKS):
        sib_copy(0, chunk, me, True).start()
    own = [pltpu.make_async_copy(shard_ref.at[:, pl.ds(chunk * width, width)],
                                 place(me, chunk), local_sem.at[chunk]) for chunk in range(CHUNKS)]
    for copy in own:
        copy.start()

    zeros = jnp.zeros((8, LANES), jnp.float32)

    def halo_copy(slot, way):
        return pltpu.make_async_remote_copy(
            src_ref=halo_out.at[slot, way], dst_ref=halo_in.at[slot, way],
            send_sem=halo_send.at[slot, way], recv_sem=halo_recv.at[slot, way],
            device_id={"cell": me - 1 if way == 0 else me + 1})

    def send_halo(state, slot):
        for way, start in ((0, first), (1, last - EDGE)):
            for c in range(4):
                halo_out[slot, way, :, c * EDGE:(c + 1) * EDGE, :] = state[c, :, start:start + EDGE, :]

        @pl.when(me > 0)
        def _():
            halo_copy(slot, 0).start()

        @pl.when(me < n - 1)
        def _():
            halo_copy(slot, 1).start()

    def take_halo(state, slot):
        @pl.when(me > 0)
        def _():
            halo_copy(slot, 0).wait_send()
            halo_copy(slot, 1).wait_recv()
            for c in range(4):
                state[c, :, first - EDGE:first, :] = halo_in[slot, 1, :, c * EDGE:(c + 1) * EDGE, :]

        @pl.when(me < n - 1)
        def _():
            halo_copy(slot, 1).wait_send()
            halo_copy(slot, 0).wait_recv()
            for c in range(4):
                state[c, :, last:last + EDGE, :] = halo_in[slot, 0, :, c * EDGE:(c + 1) * EDGE, :]

    def keep(t, parts, state, s_ref, e_ref):
        lane = pl.ds(t * LANES, LANES)
        for c in range(4):
            state[c, t, first:last, :] = parts[c]
            s_ref[c * cells:(c + 1) * cells, lane] = parts[c].astype(jnp.bfloat16)
        for c in range(2):
            e_ref[c * cells:(c + 1) * cells, lane] = (1.0 - parts[c]).astype(jnp.bfloat16)

    for state in (dens, pred):
        for c in range(4):
            for t in range(tiles):
                state[c, t, 0:8, :] = zeros
                state[c, t, last:last + 8, :] = zeros
    for t in range(tiles):
        lane = slice(t * LANES, (t + 1) * LANES)
        keep(t, [ref[:, b, lane] for ref in (pop_ref, coh_ref) for b in range(2)],
             dens, s_dens, e_dens)
    send_halo(dens, 0)

    def flip_block(row, column):
        block = kern[pl.ds(row, LANES), pl.ds(column, LANES)]
        kern_t[pl.ds(column, LANES), pl.ds(row, LANES)] = block.T

    whole_tiles = rows % LANES == 0

    def flip(device, chunk):
        if whole_tiles:
            for r in range(rows // LANES):
                for k in range(width // LANES):
                    flip_block(pl.multiple_of(device * rows + r * LANES, LANES),
                               chunk * width + k * LANES)

    for chunk in range(CHUNKS):
        own[chunk].wait()
        flip(me, chunk)

    def gather(step, _):
        for chunk in (0, 2, 1, 3):
            _, device = ring_arrival(step, chunk)
            ring_copy(step, chunk, False).wait_recv()

            @pl.when(step < chips - 2)
            def _():
                ring_copy(step + 1, chunk, False).start()

            sib_copy(step + 1, chunk, device, False).start()
            flip(device, chunk)
        for chunk in (0, 2, 1, 3):
            rightward = chunk < CHUNKS // 2
            position = (spot + chips - step) % chips if rightward else (spot + step) % chips
            device = other_core(device_at(position))
            sib_copy(step, chunk, device, False).wait_recv()
            flip(device, chunk)
        return 0

    lax.fori_loop(0, chips - 1, gather, 0)
    for chunk in (0, 2, 1, 3):
        rightward = chunk < CHUNKS // 2
        position = (spot + 1) % chips if rightward else (spot + chips - 1) % chips
        device = other_core(device_at(position))
        sib_copy(chips - 1, chunk, device, False).wait_recv()
        flip(device, chunk)

    def drain(step, _):
        for chunk in range(CHUNKS):
            @pl.when(step < chips - 1)
            def _():
                ring_copy(step, chunk, False).wait_send()

            sib_copy(step, chunk, me, False).wait_send()
        return 0

    lax.fori_loop(0, chips, drain, 0)

    if not whole_tiles:
        def flip_rows(r, _):
            for k in range(tiles):
                flip_block(pl.multiple_of(r * LANES, LANES), k * LANES)
            return 0

        lax.fori_loop(0, tiles, flip_rows, 0)

    span = momenta // BLOCKS

    def products(block, s_ref, e_ref):
        columns = slice(block * span, (block + 1) * span)
        gain[:, columns] = jnp.dot(s_ref[...], kern_t[:, columns], preferred_element_type=jnp.float32)
        loss[:, columns] = jnp.dot(e_ref[...], kern[:, columns], preferred_element_type=jnp.float32)

    def advance(block, state, finish):
        absorb = wall_ref[...]
        for t in range(block * tiles // BLOCKS, (block + 1) * tiles // BLOCKS):
            lane = slice(t * LANES, (t + 1) * LANES)
            row = [coef_ref[t, d:d + 1, :] for d in range(8)]
            detune = row[7]
            here = [state[c, t, first:last, :] for c in range(4)]
            g = [gain[c * cells:(c + 1) * cells, lane] for c in range(4)]
            l = [loss[c * cells:(c + 1) * cells, lane] for c in range(2)]
            mean_hole = 1.0 - 0.5 * (here[0] + here[1])
            damping = 0.5 * (l[0] + l[1])
            scatter = [
                (1.0 - here[0]) * g[0] - here[0] * l[0],
                (1.0 - here[1]) * g[1] - here[1] * l[1],
                mean_hole * g[2] - damping * here[2] - detune * here[3],
                mean_hole * g[3] - damping * here[3] + detune * here[2],
            ]
            moved = []
            for c in range(4):
                total = row[3] * here[c]
                for d in (0, 1, 2, 4, 5, 6):
                    total = total + row[d] * state[c, t, first - 3 + d:last - 3 + d, :]
                moved.append(total + scatter[c] - absorb * here[c])
            finish(t, here, moved)

    def stage(state, s_ref, e_ref, slot, finish):
        for block in range(BLOCKS):
            products(block, s_ref, e_ref)
            if block == 1:
                take_halo(state, slot)
            if block >= 1:
                advance(block - 1, state, finish)
        advance(BLOCKS - 1, state, finish)

    def predict(t, here, rate):
        keep(t, [here[c] + TIME_STEP * rate[c] for c in range(4)], pred, s_pred, e_pred)

    def correct(t, here, rate):
        keep(t, [0.5 * (dens[c, t, first:last, :] + here[c] + TIME_STEP * rate[c]) for c in range(4)],
             dens, s_dens, e_dens)

    def step(count, _):
        stage(dens, s_dens, e_dens, 0, predict)
        send_halo(pred, 1)
        stage(pred, s_pred, e_pred, 1, correct)

        @pl.when(count < STEPS - 1)
        def _():
            send_halo(dens, 0)

        return 0

    lax.fori_loop(0, STEPS, step, 0)
    for c in range(4):
        for t in range(tiles):
            out_ref[c, :, t * LANES:(t + 1) * LANES] = dens[c, t, first:last, :]


def on_device(populations, coherences, kernel, velocity, heading, wall_flags, detune):
    n = lax.axis_size("cell")
    cells, _, momenta = populations.shape
    tiles = momenta // LANES
    chips = n // 2
    forward = heading > 0
    scale = -velocity / 60.0
    rows = [scale * jnp.where(forward, a, b) for a, b in zip(FORWARD, BACKWARD)] + [detune]
    coef = jnp.stack([row.reshape(tiles, LANES) for row in rows], axis=1)
    wall = jnp.broadcast_to(ABSORPTION * wall_flags.astype(jnp.float32)[:, None], (cells, LANES))
    f32, bf16 = jnp.float32, jnp.bfloat16
    vmem = pltpu.VMEM
    dma = pltpu.SemaphoreType.DMA
    out = pl.pallas_call(
        functools.partial(fused, n),
        out_shape=jax.ShapeDtypeStruct((4, cells, momenta), f32),
        in_specs=[pl.BlockSpec(memory_space=vmem)] * 5,
        out_specs=pl.BlockSpec(memory_space=vmem),
        scratch_shapes=[
            vmem((momenta, momenta), bf16),
            vmem((momenta, momenta), bf16),
            vmem((4, tiles, cells + 16, LANES), f32),
            vmem((4, tiles, cells + 16, LANES), f32),
            vmem((4 * cells, momenta), bf16),
            vmem((4 * cells, momenta), bf16),
            vmem((2 * cells, momenta), bf16),
            vmem((2 * cells, momenta), bf16),
            vmem((4 * cells, momenta), f32),
            vmem((2 * cells, momenta), f32),
            vmem((2, 2, tiles, 4 * EDGE, LANES), f32),
            vmem((2, 2, tiles, 4 * EDGE, LANES), f32),
            dma((CHUNKS, chips)), dma((CHUNKS, chips)),
            dma((CHUNKS, chips)), dma((CHUNKS, chips)),
            dma((2, 2)), dma((2, 2)), dma((CHUNKS,)),
        ],
        compiler_params=pltpu.CompilerParams(
            collective_id=0, has_side_effects=True, vmem_limit_bytes=48 * 2**20),
        cost_estimate=pl.CostEstimate(
            flops=2 * STEPS * 2 * 6 * cells * momenta * momenta,
            bytes_accessed=3 * 2**20, transcendentals=0),
    )(populations, coherences, kernel, coef, wall)
    out = jnp.swapaxes(out, 0, 1)
    return out[:, :2], out[:, 2:]


def solution(mesh):
    in_specs = (
        P(("sweep", "cell"), None, None),
        P(("sweep", "cell"), None, None),
        P("cell", None),
        P(),
        P(),
        P("cell"),
        P("sweep"),
    )
    out_specs = (P(("sweep", "cell"), None, None), P(("sweep", "cell"), None, None))
    return jax.shard_map(
        on_device, mesh=mesh, in_specs=in_specs, out_specs=out_specs, check_vma=False
    )
```

```python
import functools

import jax
import jax.numpy as jnp
from jax import lax
from jax.experimental import pallas as pl
from jax.experimental.pallas import tpu as pltpu
from jax.sharding import PartitionSpec as P

STEPS = 4
TIME_STEP = 0.5
ABSORPTION = 1.0
LANES = 128
EDGE = 3
PARTS = 2
FORWARD = (-2.0, 15.0, -60.0, 20.0, 30.0, -3.0, 0.0)
BACKWARD = (0.0, 3.0, -30.0, -20.0, 60.0, -15.0, 2.0)
CHUNKS = 8
RING = 6
CROSS = 2
BLOCKS = 4


def fused(n, pop_hbm, coh_hbm, shard_ref, coef_hbm, wall_hbm, out_ref,
          pop_ref, coh_ref, coef_ref, wall_ref, kern, kern_t, dens, pred, s_dens, s_pred, e_dens, e_pred, gain, loss,
          halo_out, halo_in, ring_send, ring_recv, sib_send, sib_recv, cross_send, cross_recv,
          halo_send, halo_recv, local_sem):
    cells = pop_ref.shape[0]
    momenta = shard_ref.shape[1]
    rows = shard_ref.shape[0]
    tiles = momenta // LANES
    width = momenta // CHUNKS
    chips = n // 2
    half = chips // 2
    first = 8
    last = first + cells

    me = lax.axis_index("cell")
    sweep = lax.axis_index("sweep")
    parity = sweep % 2
    peer = {"sweep": sweep + 1 - 2 * parity, "cell": me}
    core = me % 2
    chip = me // 2
    sibling = chip * 2 + 1 - core
    odd = chip % 2
    spot = (1 - odd) * (chip // 2) + odd * (chips - 1 - chip // 2)

    def device_at(position):
        late = position // half
        at = (1 - late) * (2 * position) + late * (2 * (chips - 1 - position) + 1)
        return at * 2 + core

    right = device_at((spot + 1) % chips)
    left = device_at((spot + chips - 1) % chips)

    barrier = pltpu.get_barrier_semaphore()
    for other in (right, left, sibling, (me + 1) % n, (me + n - 1) % n):
        pl.semaphore_signal(barrier, inc=1, device_id={"cell": other})
    pl.semaphore_signal(barrier, inc=1, device_id=peer)
    pl.semaphore_wait(barrier, 6)

    def columns_of(role):
        chunk = role + parity * (CHUNKS - 1 - 2 * role)
        return pl.multiple_of(chunk * width, width)

    def place(device, role):
        return kern.at[pl.ds(pl.multiple_of(device * rows, rows), rows),
                       pl.ds(columns_of(role), width)]

    def source(distance, role):
        rightward = role % 2 == 0 if role < RING else role % 2 == 1
        if rightward:
            return device_at((spot + chips - distance) % chips)
        return device_at((spot + distance) % chips)

    def piece(distance, role, own):
        here = place(source(distance, role), role)
        return (shard_ref.at[:, pl.ds(columns_of(role), width)] if own else here), here

    def ring_copy(step, role, own=False):
        src, here = piece(step, role, own)
        return pltpu.make_async_remote_copy(
            src_ref=src, dst_ref=here,
            send_sem=ring_send.at[role, step], recv_sem=ring_recv.at[role, step],
            device_id={"cell": right if role % 2 == 0 else left})

    def sib_copy(distance, role, own=False):
        src, here = piece(distance, role, own)
        return pltpu.make_async_remote_copy(
            src_ref=src, dst_ref=here,
            send_sem=sib_send.at[role, distance], recv_sem=sib_recv.at[role, distance],
            device_id={"cell": sibling})

    def cross_copy(step, role):
        src, here = piece(step + 1, role, False)
        return pltpu.make_async_remote_copy(
            src_ref=src, dst_ref=here,
            send_sem=cross_send.at[role, step], recv_sem=cross_recv.at[role, step],
            device_id=peer)

    def other_core(device):
        return device + 1 - 2 * core

    for role in range(RING):
        ring_copy(0, role, True).start()
    own = [pltpu.make_async_copy(shard_ref.at[:, pl.ds(columns_of(role), width)],
                                 place(me, role), local_sem.at[role]) for role in range(CHUNKS)]
    loads = [pltpu.make_async_copy(src, dst, local_sem.at[CHUNKS + i]) for i, (src, dst) in enumerate(
        ((pop_hbm, pop_ref), (coh_hbm, coh_ref), (coef_hbm, coef_ref), (wall_hbm, wall_ref)))]
    for copy in loads + own:
        copy.start()
    for role in range(CHUNKS):
        sib_copy(0, role, True).start()

    zeros = jnp.zeros((8, LANES), jnp.float32)

    pairs = tiles // 2
    depth = 4 * EDGE

    def halo_copy(slot, way, part):
        some = pl.ds(part * (pairs // PARTS), pairs // PARTS)
        return pltpu.make_async_remote_copy(
            src_ref=halo_out.at[slot, way, some], dst_ref=halo_in.at[slot, way, some],
            send_sem=halo_send.at[slot, way, part], recv_sem=halo_recv.at[slot, way, part],
            device_id={"cell": me - 1 if way == 0 else me + 1})

    def edge_rows(part):
        for t in range(part * (tiles // PARTS), (part + 1) * (tiles // PARTS)):
            for c in range(4):
                row = (t % 2) * depth + c * EDGE
                yield c, t, (t // 2, slice(row, row + EDGE), slice(None))

    def send_halo(state, slot, part):
        for way, start in ((0, first), (1, last - EDGE)):
            for c, t, spot_in in edge_rows(part):
                halo_out[(slot, way) + spot_in] = state[c, t, start:start + EDGE, :]

        @pl.when(me > 0)
        def _():
            halo_copy(slot, 0, part).start()

        @pl.when(me < n - 1)
        def _():
            halo_copy(slot, 1, part).start()

    def take_halo(state, slot, part):
        @pl.when(me > 0)
        def _():
            halo_copy(slot, 0, part).wait_send()
            halo_copy(slot, 1, part).wait_recv()
            for c, t, spot_in in edge_rows(part):
                state[c, t, first - EDGE:first, :] = halo_in[(slot, 1) + spot_in]

        @pl.when(me < n - 1)
        def _():
            halo_copy(slot, 1, part).wait_send()
            halo_copy(slot, 0, part).wait_recv()
            for c, t, spot_in in edge_rows(part):
                state[c, t, last:last + EDGE, :] = halo_in[(slot, 0) + spot_in]

    inner = cells - 16

    def of_cells(read, edge):
        if edge:
            return jnp.concatenate([read(0, 8), read(cells - 8, cells)], axis=0)
        return read(8, cells - 8)

    def row_range(c, edge):
        return slice(c * cells + inner, (c + 1) * cells) if edge else slice(c * cells, c * cells + inner)

    def keep(t, edge, parts, state, s_ref, e_ref):
        lane = pl.ds(t * LANES, LANES)
        for c in range(4):
            if edge:
                state[c, t, first:first + 8, :] = parts[c][:8]
                state[c, t, last - 8:last, :] = parts[c][8:]
            else:
                state[c, t, first + 8:last - 8, :] = parts[c]
            s_ref[row_range(c, edge), lane] = parts[c].astype(jnp.bfloat16)
        for c in range(2):
            e_ref[row_range(c, edge), lane] = (1.0 - parts[c]).astype(jnp.bfloat16)

    for state in (dens, pred):
        for c in range(4):
            for t in range(tiles):
                state[c, t, 0:8, :] = zeros
                state[c, t, last:last + 8, :] = zeros
    for copy in loads:
        copy.wait()
    for t in range(tiles):
        lane = slice(t * LANES, (t + 1) * LANES)
        for edge in (False, True):
            keep(t, edge, [of_cells(lambda i, j: ref[i:j, b, lane], edge)
                           for ref in (pop_ref, coh_ref) for b in range(2)],
                 dens, s_dens, e_dens)
    for part in range(PARTS):
        send_halo(dens, 0, part)

    def flip_block(row, column):
        block = kern[pl.ds(row, LANES), pl.ds(column, LANES)]
        kern_t[pl.ds(column, LANES), pl.ds(row, LANES)] = block.T

    whole_tiles = rows % LANES == 0

    def flip(device, role):
        if whole_tiles:
            for r in range(rows // LANES):
                for k in range(width // LANES):
                    flip_block(pl.multiple_of(device * rows + r * LANES, LANES),
                               pl.multiple_of(columns_of(role) + k * LANES, LANES))

    def from_sibling(distance, roles):
        for role in roles:
            sib_copy(distance, role).wait_recv()
            flip(other_core(source(distance, role)), role)

    ring_roles, cross_roles = range(RING), range(RING, CHUNKS)

    for role in range(CHUNKS):
        own[role].wait()
        flip(me, role)

    def gather(step, _):
        for role in ring_roles:
            ring_copy(step, role).wait_recv()

            @pl.when(step < chips - 2)
            def _():
                ring_copy(step + 1, role).start()

            if role < CROSS:
                cross_copy(step, role).start()
            sib_copy(step + 1, role).start()

        @pl.when(step > 0)
        def _():
            for role in cross_roles:
                cross_copy(step - 1, CHUNKS - 1 - role).wait_recv()
                sib_copy(step, role).start()

        for role in ring_roles:
            flip(source(step + 1, role), role)
        from_sibling(step, ring_roles)

        @pl.when(step > 0)
        def _():
            for role in cross_roles:
                flip(source(step, role), role)
            from_sibling(step - 1, cross_roles)

        return 0

    lax.fori_loop(0, chips - 1, gather, 0)
    for role in cross_roles:
        cross_copy(chips - 2, CHUNKS - 1 - role).wait_recv()
        sib_copy(chips - 1, role).start()
        flip(source(chips - 1, role), role)
    from_sibling(chips - 1, ring_roles)
    from_sibling(chips - 2, cross_roles)
    from_sibling(chips - 1, cross_roles)

    def drain(step, _):
        for role in range(CHUNKS):
            sib_copy(step, role).wait_send()

        @pl.when(step < chips - 1)
        def _():
            for role in ring_roles:
                ring_copy(step, role).wait_send()
            for role in range(CROSS):
                cross_copy(step, role).wait_send()

        return 0

    lax.fori_loop(0, chips, drain, 0)

    if not whole_tiles:
        def flip_rows(r, _):
            for k in range(tiles):
                flip_block(pl.multiple_of(r * LANES, LANES), k * LANES)
            return 0

        lax.fori_loop(0, tiles, flip_rows, 0)

    span = momenta // BLOCKS

    def products(block, s_ref, e_ref):
        columns = slice(block * span, (block + 1) * span)
        gain[:, columns] = jnp.dot(s_ref[...], kern_t[:, columns], preferred_element_type=jnp.float32)
        loss[:, columns] = jnp.dot(e_ref[...], kern[:, columns], preferred_element_type=jnp.float32)

    def shifted(state, c, t, d, edge):
        return of_cells(lambda i, j: state[c, t, first + i + d:first + j + d, :], edge)

    def advance(block, state, edge, finish):
        absorb = of_cells(lambda i, j: wall_ref[i:j, :], edge)
        for t in range(block * tiles // BLOCKS, (block + 1) * tiles // BLOCKS):
            lane = slice(t * LANES, (t + 1) * LANES)
            row = [coef_ref[t, d:d + 1, :] for d in range(8)]
            detune = row[7]
            here = [shifted(state, c, t, 0, edge) for c in range(4)]
            g = [gain[row_range(c, edge), lane] for c in range(4)]
            l = [loss[row_range(c, edge), lane] for c in range(2)]
            mean_hole = 1.0 - 0.5 * (here[0] + here[1])
            damping = 0.5 * (l[0] + l[1])
            scatter = [
                (1.0 - here[0]) * g[0] - here[0] * l[0],
                (1.0 - here[1]) * g[1] - here[1] * l[1],
                mean_hole * g[2] - damping * here[2] - detune * here[3],
                mean_hole * g[3] - damping * here[3] + detune * here[2],
            ]
            moved = []
            for c in range(4):
                total = row[3] * here[c]
                for d in (0, 1, 2, 4, 5, 6):
                    total = total + row[d] * shifted(state, c, t, d - 3, edge)
                moved.append(total + scatter[c] - absorb * here[c])
            finish(t, edge, here, moved)

    def stage(state, s_ref, e_ref, slot, finish, send):
        for block in range(BLOCKS):
            products(block, s_ref, e_ref)
            if block >= 1:
                advance(block - 1, state, False, finish)
        advance(BLOCKS - 1, state, False, finish)
        for part in range(PARTS):
            take_halo(state, slot, part)
            for block in range(part * BLOCKS // PARTS, (part + 1) * BLOCKS // PARTS):
                advance(block, state, True, finish)
            send(part)

    def predict(t, edge, here, rate):
        keep(t, edge, [here[c] + TIME_STEP * rate[c] for c in range(4)], pred, s_pred, e_pred)

    def correct(t, edge, here, rate):
        keep(t, edge, [0.5 * (shifted(dens, c, t, 0, edge) + here[c] + TIME_STEP * rate[c])
                       for c in range(4)], dens, s_dens, e_dens)

    def step(count, _):
        def send_density(part):
            @pl.when(count < STEPS - 1)
            def _():
                send_halo(dens, 0, part)

        stage(dens, s_dens, e_dens, 0, predict, lambda part: send_halo(pred, 1, part))
        stage(pred, s_pred, e_pred, 1, correct, send_density)
        return 0

    lax.fori_loop(0, STEPS, step, 0)
    for c in range(4):
        for t in range(tiles):
            out_ref[c, :, t * LANES:(t + 1) * LANES] = dens[c, t, first:last, :]


def on_device(populations, coherences, kernel, velocity, heading, wall_flags, detune):
    n = lax.axis_size("cell")
    cells, _, momenta = populations.shape
    tiles = momenta // LANES
    chips = n // 2
    forward = heading > 0
    scale = -velocity / 60.0
    rows = [scale * jnp.where(forward, a, b) for a, b in zip(FORWARD, BACKWARD)] + [detune]
    coef = jnp.stack([row.reshape(tiles, LANES) for row in rows], axis=1)
    wall = jnp.broadcast_to(ABSORPTION * wall_flags.astype(jnp.float32)[:, None], (cells, LANES))
    f32, bf16 = jnp.float32, jnp.bfloat16
    vmem = pltpu.VMEM
    dma = pltpu.SemaphoreType.DMA
    out = pl.pallas_call(
        functools.partial(fused, n),
        out_shape=jax.ShapeDtypeStruct((4, cells, momenta), f32),
        in_specs=[pl.BlockSpec(memory_space=pltpu.HBM)] * 5,
        out_specs=pl.BlockSpec(memory_space=vmem),
        scratch_shapes=[
            vmem(populations.shape, f32),
            vmem(coherences.shape, f32),
            vmem(coef.shape, f32),
            vmem(wall.shape, f32),
            vmem((momenta, momenta), bf16),
            vmem((momenta, momenta), bf16),
            vmem((4, tiles, cells + 16, LANES), f32),
            vmem((4, tiles, cells + 16, LANES), f32),
            vmem((4 * cells, momenta), bf16),
            vmem((4 * cells, momenta), bf16),
            vmem((2 * cells, momenta), bf16),
            vmem((2 * cells, momenta), bf16),
            vmem((4 * cells, momenta), f32),
            vmem((2 * cells, momenta), f32),
            vmem((2, 2, tiles // 2, 8 * EDGE, LANES), f32),
            vmem((2, 2, tiles // 2, 8 * EDGE, LANES), f32),
            dma((RING, chips)), dma((RING, chips)),
            dma((CHUNKS, chips)), dma((CHUNKS, chips)),
            dma((CROSS, chips)), dma((CROSS, chips)),
            dma((2, 2, PARTS)), dma((2, 2, PARTS)), dma((CHUNKS + 4,)),
        ],
        compiler_params=pltpu.CompilerParams(
            collective_id=0, has_side_effects=True, vmem_limit_bytes=48 * 2**20),
        cost_estimate=pl.CostEstimate(
            flops=2 * STEPS * 2 * 6 * cells * momenta * momenta,
            bytes_accessed=3 * 2**20, transcendentals=0),
    )(populations, coherences, kernel, coef, wall)
    out = jnp.swapaxes(out, 0, 1)
    return out[:, :2], out[:, 2:]


def solution(mesh):
    in_specs = (
        P(("sweep", "cell"), None, None),
        P(("sweep", "cell"), None, None),
        P("cell", None),
        P(),
        P(),
        P("cell"),
        P("sweep"),
    )
    out_specs = (P(("sweep", "cell"), None, None), P(("sweep", "cell"), None, None))
    return jax.shard_map(
        on_device, mesh=mesh, in_specs=in_specs, out_specs=out_specs, check_vma=False
    )
```

```python
import functools

import jax
import jax.numpy as jnp
from jax import lax
from jax.experimental import pallas as pl
from jax.experimental.pallas import tpu as pltpu
from jax.sharding import PartitionSpec as P

STEPS = 4
TIME_STEP = 0.5
ABSORPTION = 1.0
LANES = 128
EDGE = 3
PARTS = 2
FORWARD = (-2.0, 15.0, -60.0, 20.0, 30.0, -3.0, 0.0)
BACKWARD = (0.0, 3.0, -30.0, -20.0, 60.0, -15.0, 2.0)
CHUNKS = 8
RING = 6
CROSS = 2
BLOCKS = 2


def fused(n, pop_hbm, coh_hbm, shard_ref, coef_hbm, wall_hbm, out_ref,
          pop_ref, coh_ref, coef_ref, wall_ref, kern, kern_t, dens, pred, s_dens, s_pred, e_dens, e_pred, gain, loss,
          halo_out, halo_in, ring_send, ring_recv, sib_send, sib_recv, cross_send, cross_recv,
          halo_send, halo_recv, local_sem):
    cells = pop_ref.shape[0]
    momenta = shard_ref.shape[1]
    rows = shard_ref.shape[0]
    tiles = momenta // LANES
    width = momenta // CHUNKS
    chips = n // 2
    half = chips // 2
    first = 8
    last = first + cells

    me = lax.axis_index("cell")
    sweep = lax.axis_index("sweep")
    parity = sweep % 2
    peer = {"sweep": sweep + 1 - 2 * parity, "cell": me}
    core = me % 2
    chip = me // 2
    sibling = chip * 2 + 1 - core
    odd = chip % 2
    spot = (1 - odd) * (chip // 2) + odd * (chips - 1 - chip // 2)

    def device_at(position):
        late = position // half
        at = (1 - late) * (2 * position) + late * (2 * (chips - 1 - position) + 1)
        return at * 2 + core

    right = device_at((spot + 1) % chips)
    left = device_at((spot + chips - 1) % chips)

    barrier = pltpu.get_barrier_semaphore()
    for other in (right, left, sibling, (me + 1) % n, (me + n - 1) % n):
        pl.semaphore_signal(barrier, inc=1, device_id={"cell": other})
    pl.semaphore_signal(barrier, inc=1, device_id=peer)
    pl.semaphore_wait(barrier, 6)

    def columns_of(role):
        chunk = role + parity * (CHUNKS - 1 - 2 * role)
        return pl.multiple_of(chunk * width, width)

    def place(device, role):
        return kern.at[pl.ds(pl.multiple_of(device * rows, rows), rows),
                       pl.ds(columns_of(role), width)]

    def source(distance, role):
        rightward = role % 2 == 0 if role < RING else role % 2 == 1
        if rightward:
            return device_at((spot + chips - distance) % chips)
        return device_at((spot + distance) % chips)

    def piece(distance, role, own):
        here = place(source(distance, role), role)
        return (shard_ref.at[:, pl.ds(columns_of(role), width)] if own else here), here

    def ring_copy(step, role, own=False):
        src, here = piece(step, role, own)
        return pltpu.make_async_remote_copy(
            src_ref=src, dst_ref=here,
            send_sem=ring_send.at[role, step], recv_sem=ring_recv.at[role, step],
            device_id={"cell": right if role % 2 == 0 else left})

    def sib_copy(distance, role, own=False):
        src, here = piece(distance, role, own)
        return pltpu.make_async_remote_copy(
            src_ref=src, dst_ref=here,
            send_sem=sib_send.at[role, distance], recv_sem=sib_recv.at[role, distance],
            device_id={"cell": sibling})

    def cross_copy(step, role):
        src, here = piece(step + 1, role, False)
        return pltpu.make_async_remote_copy(
            src_ref=src, dst_ref=here,
            send_sem=cross_send.at[role, step], recv_sem=cross_recv.at[role, step],
            device_id=peer)

    def other_core(device):
        return device + 1 - 2 * core

    for role in range(RING):
        ring_copy(0, role, True).start()
    own = [pltpu.make_async_copy(shard_ref.at[:, pl.ds(columns_of(role), width)],
                                 place(me, role), local_sem.at[role]) for role in range(CHUNKS)]
    loads = [pltpu.make_async_copy(src, dst, local_sem.at[CHUNKS + i]) for i, (src, dst) in enumerate(
        ((pop_hbm, pop_ref), (coh_hbm, coh_ref), (coef_hbm, coef_ref), (wall_hbm, wall_ref)))]
    for copy in loads + own:
        copy.start()
    for role in range(CHUNKS):
        sib_copy(0, role, True).start()

    zeros = jnp.zeros((8, LANES), jnp.float32)

    pairs = tiles // 2
    depth = 4 * EDGE

    def halo_copy(slot, way, part):
        some = pl.ds(part * (pairs // PARTS), pairs // PARTS)
        return pltpu.make_async_remote_copy(
            src_ref=halo_out.at[slot, way, some], dst_ref=halo_in.at[slot, way, some],
            send_sem=halo_send.at[slot, way, part], recv_sem=halo_recv.at[slot, way, part],
            device_id={"cell": me - 1 if way == 0 else me + 1})

    def edge_rows(part):
        for t in range(part * (tiles // PARTS), (part + 1) * (tiles // PARTS)):
            for c in range(4):
                row = (t % 2) * depth + c * EDGE
                yield c, t, (t // 2, slice(row, row + EDGE), slice(None))

    def send_halo(state, slot, part):
        for way, start in ((0, first), (1, last - EDGE)):
            for c, t, spot_in in edge_rows(part):
                halo_out[(slot, way) + spot_in] = state[c, t, start:start + EDGE, :]

        @pl.when(me > 0)
        def _():
            halo_copy(slot, 0, part).start()

        @pl.when(me < n - 1)
        def _():
            halo_copy(slot, 1, part).start()

    def take_halo(state, slot, part):
        @pl.when(me > 0)
        def _():
            halo_copy(slot, 0, part).wait_send()
            halo_copy(slot, 1, part).wait_recv()
            for c, t, spot_in in edge_rows(part):
                state[c, t, first - EDGE:first, :] = halo_in[(slot, 1) + spot_in]

        @pl.when(me < n - 1)
        def _():
            halo_copy(slot, 1, part).wait_send()
            halo_copy(slot, 0, part).wait_recv()
            for c, t, spot_in in edge_rows(part):
                state[c, t, last:last + EDGE, :] = halo_in[(slot, 0) + spot_in]

    inner = cells - 16

    def of_cells(read, edge):
        if edge:
            return jnp.concatenate([read(0, 8), read(cells - 8, cells)], axis=0)
        return read(8, cells - 8)

    def row_range(c, edge):
        return slice(c * cells + inner, (c + 1) * cells) if edge else slice(c * cells, c * cells + inner)

    def keep(t, edge, parts, state, s_ref, e_ref):
        lane = pl.ds(t * LANES, LANES)
        for c in range(4):
            if edge:
                state[c, t, first:first + 8, :] = parts[c][:8]
                state[c, t, last - 8:last, :] = parts[c][8:]
            else:
                state[c, t, first + 8:last - 8, :] = parts[c]
            s_ref[row_range(c, edge), lane] = parts[c].astype(jnp.bfloat16)
        for c in range(2):
            e_ref[row_range(c, edge), lane] = (1.0 - parts[c]).astype(jnp.bfloat16)

    for state in (dens, pred):
        for c in range(4):
            for t in range(tiles):
                state[c, t, 0:8, :] = zeros
                state[c, t, last:last + 8, :] = zeros
    for copy in loads:
        copy.wait()
    for t in range(tiles):
        lane = slice(t * LANES, (t + 1) * LANES)
        for edge in (False, True):
            keep(t, edge, [of_cells(lambda i, j: ref[i:j, b, lane], edge)
                           for ref in (pop_ref, coh_ref) for b in range(2)],
                 dens, s_dens, e_dens)
    for part in range(PARTS):
        send_halo(dens, 0, part)

    def flip_block(row, column):
        block = kern[pl.ds(row, LANES), pl.ds(column, LANES)]
        kern_t[pl.ds(column, LANES), pl.ds(row, LANES)] = block.T

    whole_tiles = rows % LANES == 0

    def flip(device, role):
        if whole_tiles:
            for r in range(rows // LANES):
                for k in range(width // LANES):
                    flip_block(pl.multiple_of(device * rows + r * LANES, LANES),
                               pl.multiple_of(columns_of(role) + k * LANES, LANES))

    def from_sibling(distance, roles):
        for role in roles:
            sib_copy(distance, role).wait_recv()
            flip(other_core(source(distance, role)), role)

    ring_roles, cross_roles = range(RING), range(RING, CHUNKS)

    for role in range(CHUNKS):
        own[role].wait()
        flip(me, role)

    def gather(step, _):
        for role in ring_roles:
            ring_copy(step, role).wait_recv()

            @pl.when(step < chips - 2)
            def _():
                ring_copy(step + 1, role).start()

            if role < CROSS:
                cross_copy(step, role).start()
            sib_copy(step + 1, role).start()

        @pl.when(step > 0)
        def _():
            for role in cross_roles:
                cross_copy(step - 1, CHUNKS - 1 - role).wait_recv()
                sib_copy(step, role).start()

        for role in ring_roles:
            flip(source(step + 1, role), role)
        from_sibling(step, ring_roles)

        @pl.when(step > 0)
        def _():
            for role in cross_roles:
                flip(source(step, role), role)
            from_sibling(step - 1, cross_roles)

        return 0

    lax.fori_loop(0, chips - 1, gather, 0)
    for role in cross_roles:
        cross_copy(chips - 2, CHUNKS - 1 - role).wait_recv()
        sib_copy(chips - 1, role).start()
        flip(source(chips - 1, role), role)
    from_sibling(chips - 1, ring_roles)
    from_sibling(chips - 2, cross_roles)
    from_sibling(chips - 1, cross_roles)

    def drain(step, _):
        for role in range(CHUNKS):
            sib_copy(step, role).wait_send()

        @pl.when(step < chips - 1)
        def _():
            for role in ring_roles:
                ring_copy(step, role).wait_send()
            for role in range(CROSS):
                cross_copy(step, role).wait_send()

        return 0

    lax.fori_loop(0, chips, drain, 0)

    if not whole_tiles:
        def flip_rows(r, _):
            for k in range(tiles):
                flip_block(pl.multiple_of(r * LANES, LANES), k * LANES)
            return 0

        lax.fori_loop(0, tiles, flip_rows, 0)

    span = momenta // BLOCKS

    def products(block, s_ref, e_ref):
        columns = slice(block * span, (block + 1) * span)
        gain[:, columns] = jnp.dot(s_ref[...], kern_t[:, columns], preferred_element_type=jnp.float32)
        loss[:, columns] = jnp.dot(e_ref[...], kern[:, columns], preferred_element_type=jnp.float32)

    def shifted(state, c, t, d, edge):
        return of_cells(lambda i, j: state[c, t, first + i + d:first + j + d, :], edge)

    def advance(block, state, edge, finish):
        absorb = of_cells(lambda i, j: wall_ref[i:j, :], edge)
        for t in range(block * tiles // BLOCKS, (block + 1) * tiles // BLOCKS):
            lane = slice(t * LANES, (t + 1) * LANES)
            row = [coef_ref[t, d:d + 1, :] for d in range(8)]
            detune = row[7]
            here = [shifted(state, c, t, 0, edge) for c in range(4)]
            g = [gain[row_range(c, edge), lane] for c in range(4)]
            l = [loss[row_range(c, edge), lane] for c in range(2)]
            mean_hole = 1.0 - 0.5 * (here[0] + here[1])
            damping = 0.5 * (l[0] + l[1])
            scatter = [
                (1.0 - here[0]) * g[0] - here[0] * l[0],
                (1.0 - here[1]) * g[1] - here[1] * l[1],
                mean_hole * g[2] - damping * here[2] - detune * here[3],
                mean_hole * g[3] - damping * here[3] + detune * here[2],
            ]
            moved = []
            for c in range(4):
                total = row[3] * here[c]
                for d in (0, 1, 2, 4, 5, 6):
                    total = total + row[d] * shifted(state, c, t, d - 3, edge)
                moved.append(total + scatter[c] - absorb * here[c])
            finish(t, edge, here, moved)

    def stage(state, s_ref, e_ref, slot, finish, send):
        for block in range(BLOCKS):
            products(block, s_ref, e_ref)
            if block >= 1:
                advance(block - 1, state, False, finish)
        advance(BLOCKS - 1, state, False, finish)
        for part in range(PARTS):
            take_halo(state, slot, part)
            for block in range(part * BLOCKS // PARTS, (part + 1) * BLOCKS // PARTS):
                advance(block, state, True, finish)
            send(part)

    def predict(t, edge, here, rate):
        keep(t, edge, [here[c] + TIME_STEP * rate[c] for c in range(4)], pred, s_pred, e_pred)

    def correct(t, edge, here, rate):
        keep(t, edge, [0.5 * (shifted(dens, c, t, 0, edge) + here[c] + TIME_STEP * rate[c])
                       for c in range(4)], dens, s_dens, e_dens)

    def step(count, _):
        def send_density(part):
            @pl.when(count < STEPS - 1)
            def _():
                send_halo(dens, 0, part)

        stage(dens, s_dens, e_dens, 0, predict, lambda part: send_halo(pred, 1, part))
        stage(pred, s_pred, e_pred, 1, correct, send_density)
        return 0

    lax.fori_loop(0, STEPS, step, 0)
    for c in range(4):
        for t in range(tiles):
            out_ref[c, :, t * LANES:(t + 1) * LANES] = dens[c, t, first:last, :]


def on_device(populations, coherences, kernel, velocity, heading, wall_flags, detune):
    n = lax.axis_size("cell")
    cells, _, momenta = populations.shape
    tiles = momenta // LANES
    chips = n // 2
    forward = heading > 0
    scale = -velocity / 60.0
    rows = [scale * jnp.where(forward, a, b) for a, b in zip(FORWARD, BACKWARD)] + [detune]
    coef = jnp.stack([row.reshape(tiles, LANES) for row in rows], axis=1)
    wall = jnp.broadcast_to(ABSORPTION * wall_flags.astype(jnp.float32)[:, None], (cells, LANES))
    f32, bf16 = jnp.float32, jnp.bfloat16
    vmem = pltpu.VMEM
    dma = pltpu.SemaphoreType.DMA
    out = pl.pallas_call(
        functools.partial(fused, n),
        out_shape=jax.ShapeDtypeStruct((4, cells, momenta), f32),
        in_specs=[pl.BlockSpec(memory_space=pltpu.HBM)] * 5,
        out_specs=pl.BlockSpec(memory_space=vmem),
        scratch_shapes=[
            vmem(populations.shape, f32),
            vmem(coherences.shape, f32),
            vmem(coef.shape, f32),
            vmem(wall.shape, f32),
            vmem((momenta, momenta), bf16),
            vmem((momenta, momenta), bf16),
            vmem((4, tiles, cells + 16, LANES), f32),
            vmem((4, tiles, cells + 16, LANES), f32),
            vmem((4 * cells, momenta), bf16),
            vmem((4 * cells, momenta), bf16),
            vmem((2 * cells, momenta), bf16),
            vmem((2 * cells, momenta), bf16),
            vmem((4 * cells, momenta), f32),
            vmem((2 * cells, momenta), f32),
            vmem((2, 2, tiles // 2, 8 * EDGE, LANES), f32),
            vmem((2, 2, tiles // 2, 8 * EDGE, LANES), f32),
            dma((RING, chips)), dma((RING, chips)),
            dma((CHUNKS, chips)), dma((CHUNKS, chips)),
            dma((CROSS, chips)), dma((CROSS, chips)),
            dma((2, 2, PARTS)), dma((2, 2, PARTS)), dma((CHUNKS + 4,)),
        ],
        compiler_params=pltpu.CompilerParams(
            collective_id=0, has_side_effects=True, vmem_limit_bytes=48 * 2**20),
        cost_estimate=pl.CostEstimate(
            flops=2 * STEPS * 2 * 6 * cells * momenta * momenta,
            bytes_accessed=3 * 2**20, transcendentals=0),
    )(populations, coherences, kernel, coef, wall)
    out = jnp.swapaxes(out, 0, 1)
    return out[:, :2], out[:, 2:]


def solution(mesh):
    in_specs = (
        P(("sweep", "cell"), None, None),
        P(("sweep", "cell"), None, None),
        P("cell", None),
        P(),
        P(),
        P("cell"),
        P("sweep"),
    )
    out_specs = (P(("sweep", "cell"), None, None), P(("sweep", "cell"), None, None))
    return jax.shard_map(
        on_device, mesh=mesh, in_specs=in_specs, out_specs=out_specs, check_vma=False
    )
```
